32 devices in a mesh: groups: 2 (over y), ctx: 4 (over z), exp: 2 (over x), tp: 2 (over core).
Axes of the slice: x: 2, y: 2, z: 4, core: 2. Of those that a mesh axis runs over, the one named last changes fastest.
Arguments:
- tokens: bfloat16 [4096, 6144], P(('groups', 'ctx', 'tp'), 'exp'), parts along dimension 0, may hold values from -6 to 6
- cotangent: bfloat16 [4096, 6144], P(('groups', 'ctx', 'tp'), 'exp'), parts along dimension 0, may hold values from -6 to 6
- route_logits: float32 [4096, 2], P(('groups', 'ctx', 'tp')), parts along dimension 0, may hold values from -6 to 6
- expert_ids: int32 [4096, 2], P(('groups', 'ctx', 'tp')), parts along dimension 0, may hold values from 0 to 7, as said below
- w_gate: bfloat16 [8192, 6144], P(('ctx', 'tp'), 'exp'), may hold values from -0.078125 to 0.078125
- w_up: bfloat16 [8192, 6144], P(('ctx', 'tp'), 'exp'), may hold values from -0.078125 to 0.078125
- w_down: bfloat16 [8192, 6144], P(('ctx', 'tp'), 'exp'), may hold values from -0.0625 to 0.0625
Outputs:
- token_grad: bfloat16 [4096, 6144], P(('groups', 'ctx', 'tp'), 'exp'), parts along dimension 0
- logit_grad: float32 [4096, 2], P(('groups', 'ctx', 'tp')), parts along dimension 0
- gate_grad: bfloat16 [16384, 6144], P(('groups', 'ctx', 'tp'), 'exp'), parts along dimension 0
- up_grad: bfloat16 [16384, 6144], P(('groups', 'ctx', 'tp'), 'exp'), parts along dimension 0
- down_grad: bfloat16 [16384, 6144], P(('groups', 'ctx', 'tp'), 'exp'), parts along dimension 0
The draws below stay inside these ranges and needn't reach their ends.
There are 2 independent parts, one for each index of `groups`. The reference program is written for one: setup_inputs(seed, part) draws one part's arguments, and reference() takes and returns one part's arrays. A program takes and returns all parts, laid end to end along the dimension named above; an argument that names none is the same for every part. Nothing has to cross between parts.
Inputs may be any that keep to these rules, and one draw needn't show every extreme that they name: `expert_ids`: the two experts of a token differ. In each aligned block of 256 rows (the rows of one device) at most 32 rows name expert 0, and in every draw some block has exactly 32 such rows.
All inputs are finite; a program needn't handle non-finite values.
Results may differ from the reference program's by a relative error of at most 0.013.
Values may be sent and summed in bfloat16 or wider, within the bound.
A program may use at most 128 MiB of HBM per device.

```python
import jax
import jax.numpy as jnp

D = 6144
EXPERTS = 8
FF = 8192
TOK_DEV = 256
CAP = 32
TOKENS = 2048


def draw_expert_ids(key, part):
    key = jax.random.fold_in(key, 11)
    keys = jax.random.split(key, 6)
    block_count = TOKENS // TOK_DEV
    counts = jax.random.randint(keys[0], (block_count,), 0, CAP + 1)
    full_block = jax.random.randint(keys[1], (), 0, block_count)
    counts = jnp.where(jnp.arange(block_count) == full_block, CAP, counts)
    block_keys = jax.random.split(keys[2], block_count)
    orders = jax.vmap(lambda one: jax.random.permutation(one, TOK_DEV))(block_keys)
    picked = orders < counts[:, None]
    column = jax.random.randint(keys[3], (block_count, TOK_DEV), 0, 2)
    first = jax.random.randint(keys[4], (block_count, TOK_DEV), 1, EXPERTS)
    offset = jax.random.randint(keys[5], (block_count, TOK_DEV), 1, EXPERTS - 1)
    other = 1 + (first - 1 + offset) % (EXPERTS - 1)
    left = jnp.where(picked, jnp.where(column == 0, 0, first), first)
    right = jnp.where(picked, jnp.where(column == 0, first, 0), other)
    return jnp.stack([left, right], axis=-1).reshape(TOKENS, 2).astype(jnp.int32)


def level_of(own_key, dims, shards, least, top_value):
    def one(axis_at, parts):
        draws = jax.random.uniform(jax.random.fold_in(jax.random.fold_in(own_key, 6), axis_at), (parts,), jnp.float32, least / len(shards), top_value / len(shards))
        return jnp.repeat(jnp.exp(draws), dims[axis_at] // parts).reshape((-1,) + (1,) * (len(dims) - axis_at - 1))

    factor_of = one(*shards[0])
    for cut in shards[1:]:
        factor_of = factor_of * one(*cut)
    return factor_of


def bell_draw(rng, extent, deviation, reach, cuts=(), held_as=jnp.bfloat16):
    level = level_of(rng, extent, cuts, -0.22, 0.18) if cuts else 1.0
    drawn = jax.random.normal(rng, extent, jnp.float32) * deviation * level
    return jnp.minimum(jnp.maximum(drawn, -reach), reach).astype(held_as)


def setup_inputs(seed: int = 0, part: int = 0) -> dict:
    key_list = jax.random.split(jax.random.key(seed), 8)
    part_keys = jax.random.split(jax.random.fold_in(key_list[7], part), 8)
    return {
        "tokens": bell_draw(part_keys[0], (TOKENS, D), 1.0, 6.0, ((0, 8), (1, 2))),
        "cotangent": bell_draw(part_keys[1], (TOKENS, D), 1.0, 6.0, ((0, 8), (1, 2))),
        "route_logits": bell_draw(part_keys[2], (TOKENS, 2), 1.5, 6.0, ((0, 8),), jnp.float32),
        "expert_ids": draw_expert_ids(jax.random.fold_in(jax.random.fold_in(key_list[7], part), 71), part),
        "w_gate": bell_draw(key_list[4], (FF, D), D ** -0.5, 0.078125, ((0, 8), (1, 2))),
        "w_up": bell_draw(key_list[5], (FF, D), D ** -0.5, 0.078125, ((0, 8), (1, 2))),
        "w_down": bell_draw(key_list[6], (FF, D), FF ** -0.5, 0.0625, ((0, 8), (1, 2))),
    }


def route_weights(route_logits):
    first = jax.nn.sigmoid(route_logits[:, 0] - route_logits[:, 1])
    second = jax.nn.sigmoid(route_logits[:, 1] - route_logits[:, 0])
    return jnp.stack([first, second], axis=1)


def slot_index(expert_ids):
    chosen_int = jnp.any(expert_ids == 0, axis=1).astype(jnp.int32)
    blocks = chosen_int.reshape(-1, TOK_DEV)
    position = (jnp.cumsum(blocks, axis=1) - blocks).astype(jnp.int32)
    base = jnp.arange(blocks.shape[0], dtype=jnp.int32)[:, None] * CAP
    return chosen_int.astype(jnp.int32) == 1, (base + position).reshape(-1).astype(jnp.int32)


def reference(tokens, cotangent, route_logits, expert_ids, w_gate, w_up, w_down):
    slot_count = (TOKENS // TOK_DEV) * CAP
    shares = route_weights(route_logits)
    hit_mask = expert_ids == 0
    chosen, slot_ids = slot_index(expert_ids)
    token_share = jnp.sum(jnp.where(hit_mask, shares, 0.0), axis=1).astype(jnp.bfloat16)
    target = jnp.where(chosen, slot_ids, slot_count).astype(jnp.int32)
    x_slots = jnp.zeros((slot_count, D), jnp.bfloat16).at[target].set(tokens, mode="drop")
    dy_slots = jnp.zeros((slot_count, D), jnp.bfloat16).at[target].set(cotangent, mode="drop")
    share_slots = jnp.zeros((slot_count,), jnp.bfloat16).at[target].set(token_share, mode="drop")
    share_f = share_slots.astype(jnp.float32)[:, None]
    gate_pre = jnp.dot(x_slots, w_gate.T, preferred_element_type=jnp.float32)
    up_pre = jnp.dot(x_slots, w_up.T, preferred_element_type=jnp.float32)
    back = jnp.dot(dy_slots, w_down.T, preferred_element_type=jnp.float32)
    sig_gate = jax.nn.sigmoid(gate_pre)
    activated = gate_pre * sig_gate
    hidden = (activated * up_pre).astype(jnp.bfloat16)
    weighted = (share_f * hidden.astype(jnp.float32)).astype(jnp.bfloat16)
    score = jnp.sum(hidden.astype(jnp.float32) * back, axis=1)
    hidden_back = share_f * back
    gate_back = (hidden_back * up_pre * sig_gate * (1.0 + gate_pre * (1.0 - sig_gate))).astype(jnp.bfloat16)
    up_back = (hidden_back * activated).astype(jnp.bfloat16)
    slot_grad = (jnp.dot(gate_back, w_gate, preferred_element_type=jnp.float32)
                 + jnp.dot(up_back, w_up, preferred_element_type=jnp.float32)).astype(jnp.bfloat16)
    source_row = jnp.where(chosen, slot_ids, 0).astype(jnp.int32)
    token_grad = jnp.where(chosen[:, None], slot_grad[source_row], jnp.zeros((), jnp.bfloat16))
    token_score = jnp.where(chosen, score[source_row], 0.0)
    score_terms = jnp.where(hit_mask, token_score[:, None], 0.0)
    mean_score = jnp.sum(shares * score_terms, axis=1, keepdims=True)
    logit_grad = shares * (score_terms - mean_score)
    gate_grad = jnp.dot(gate_back.T, x_slots, preferred_element_type=jnp.float32).astype(jnp.bfloat16)
    up_grad = jnp.dot(up_back.T, x_slots, preferred_element_type=jnp.float32).astype(jnp.bfloat16)
    down_grad = jnp.dot(weighted.T, dy_slots, preferred_element_type=jnp.float32).astype(jnp.bfloat16)
    return token_grad, logit_grad, gate_grad, up_grad, down_grad
```

```python
import functools

import jax
import jax.numpy as jnp
from jax import lax
from jax.experimental import pallas as pl
from jax.experimental.pallas import tpu as pltpu
from jax.sharding import PartitionSpec as P

CAP = 32
PAIR = 2 * CAP
LANES = 128
MESH = pl.DeviceIdType.MESH
F32 = jnp.float32
BF16 = jnp.bfloat16


def dot(left, right, contract):
    return lax.dot_general(
        left, right, ((contract[:1], contract[1:]), ((), ())), preferred_element_type=F32
    )


def routing(ids_ref, logits_ref):
    tokens = ids_ref.shape[1]
    hit_0, hit_1 = ids_ref[0:1, :] == 0, ids_ref[1:2, :] == 0
    chosen = jnp.where(hit_0 | hit_1, 1.0, 0.0)
    earlier = lax.broadcasted_iota(jnp.int32, (tokens, tokens), 0) < lax.broadcasted_iota(
        jnp.int32, (tokens, tokens), 1
    )
    position = dot(
        jnp.broadcast_to(chosen, (16, tokens)).astype(BF16),
        jnp.where(earlier, 1.0, 0.0).astype(BF16),
        (1, 0),
    )[0:1, :]
    slot = lax.broadcasted_iota(jnp.int32, (CAP, tokens), 0).astype(F32)
    pick = jnp.where(slot == position, 1.0, 0.0) * chosen
    gap = logits_ref[0:1, :] - logits_ref[1:2, :]
    return pick, (hit_0, hit_1), (jax.nn.sigmoid(gap), jax.nn.sigmoid(-gap))


def split_score(score):
    high = score.astype(BF16)
    return high, (score - high.astype(F32)).astype(BF16)


def exchange_kernel(
    n, n_exp,
    ids_ref, logits_ref, tok_hbm, cot_hbm, wg_hbm, wu_hbm, wd_hbm,
    xdy_out, act_out, sg_ref, score_ref,
    tok, cot, wg, wu, wd, xdy, part, psend, precv, act, grad, sib_out, sib_in, rs_out, rs_in, acc,
    load_sem, ag_send, ag_recv, sib_send, sib_recv, x_send, x_recv,
    gs_send, gs_recv, rs_send, rs_recv, xo_sem, ao_sem,
):
    c, e, tp = lax.axis_index("ctx"), lax.axis_index("exp"), lax.axis_index("tp")
    sib = 1 - tp
    width = wg.shape[1]
    ff = wg.shape[0]
    ff_tile = min(ff, 256)
    col_tile = 512 if width % 512 == 0 else 256

    loads = [
        pltpu.make_async_copy(src, dst, load_sem.at[i])
        for i, (src, dst) in enumerate(
            ((tok_hbm, tok), (cot_hbm, cot), (wg_hbm, wg), (wu_hbm, wu), (wd_hbm, wd))
        )
    ]
    for load in loads[:2]:
        load.start()

    barrier = pltpu.get_barrier_semaphore()
    for step in range(1, n):
        pl.semaphore_signal(
            barrier, inc=1, device_id={"ctx": lax.rem(c + step, n)}, device_id_type=MESH
        )
    for step in range(1, n_exp):
        pl.semaphore_signal(
            barrier, inc=1, device_id={"exp": lax.rem(e + step, n_exp)}, device_id_type=MESH
        )
    pl.semaphore_signal(barrier, inc=1, device_id={"tp": sib}, device_id_type=MESH)

    def half(j, which):
        return pl.ds(pl.multiple_of(j * PAIR + which * CAP, CAP), CAP)

    def pair(j):
        return pl.ds(pl.multiple_of(j * PAIR, PAIR), PAIR)

    def block_half(which):
        return pl.ds(pl.multiple_of(which * CAP, CAP), CAP)

    def gather_copy(j, side):
        to = jnp.where(c + 1 < n, c + 1, 0) if side == 1 else jnp.where(c > 0, c - 1, n - 1)
        return pltpu.make_async_remote_copy(
            src_ref=xdy.at[half(j, tp)], dst_ref=xdy.at[half(j, tp)],
            send_sem=ag_send.at[j, side], recv_sem=ag_recv.at[j],
            device_id={"ctx": to}, device_id_type=MESH,
        )

    def twin_copy(j, which):
        return pltpu.make_async_remote_copy(
            src_ref=xdy.at[half(j, which)], dst_ref=xdy.at[half(j, which)],
            send_sem=sib_send.at[j], recv_sem=sib_recv.at[j],
            device_id={"tp": sib}, device_id_type=MESH,
        )

    def partial_copy(j, i, step):
        return pltpu.make_async_remote_copy(
            src_ref=psend.at[i, pair(j)], dst_ref=precv.at[step - 1, i, pair(j)],
            send_sem=x_send.at[step - 1, i, j], recv_sem=x_recv.at[step - 1, i, j],
            device_id={"exp": lax.rem(e + step, n_exp)}, device_id_type=MESH,
        )

    def pair_sum_copy(j):
        return pltpu.make_async_remote_copy(
            src_ref=sib_out.at[j], dst_ref=sib_in.at[j],
            send_sem=gs_send.at[j], recv_sem=gs_recv.at[j],
            device_id={"tp": sib}, device_id_type=MESH,
        )

    def home_copy(j, source):
        return pltpu.make_async_remote_copy(
            src_ref=rs_out.at[j], dst_ref=rs_in.at[source],
            send_sem=rs_send.at[j], recv_sem=rs_recv.at[source],
            device_id={"ctx": j}, device_id_type=MESH,
        )

    def xdy_store(j):
        return pltpu.make_async_copy(xdy.at[pair(j)], xdy_out.at[pair(j)], xo_sem.at[j])

    def act_store(j):
        return pltpu.make_async_copy(act.at[pair(j)], act_out.at[pair(j)], ao_sem.at[j])

    pick, hits, shares = routing(ids_ref, logits_ref)
    token_share = jnp.where(hits[0], shares[0], 0.0) + jnp.where(hits[1], shares[1], 0.0)
    token_share = token_share.astype(BF16).astype(F32)
    share = jnp.sum(pick * token_share, axis=1, keepdims=True)
    mine = half(c, tp)
    xdy[mine, 2 * width:] = jnp.broadcast_to(share, (CAP, LANES)).astype(BF16)
    pick = pick.astype(BF16)
    for which, ref in enumerate((tok, cot)):
        loads[which].wait()
        for at in range(0, width, col_tile):
            xdy[mine, which * width + at:which * width + at + col_tile] = dot(
                pick, ref[:, at:at + col_tile], (1, 0)
            ).astype(BF16)

    for load in loads[2:]:
        load.start()
    pl.semaphore_wait(barrier, n + n_exp - 1)

    @pl.when(c + 1 < n)
    def _():
        gather_copy(c, 1).start()

    @pl.when(c > 0)
    def _():
        gather_copy(c, 0).start()

    twin_copy(c, tp).start()

    both = jnp.where(2 * c <= n - 1, c, n - 1 - c)

    def nth(k):
        near = c + jnp.where(k % 2 == 0, 1, -1) * ((k + 1) // 2)
        far = jnp.where(2 * c <= n - 1, k, n - 1 - k)
        return jnp.where(k <= 2 * both, near, far)

    def arrive(j):
        gather_copy(j, 1).wait_recv()

        @pl.when((j < c) & (c + 1 < n))
        def _():
            gather_copy(j, 1).start()

        @pl.when((j > c) & (c > 0))
        def _():
            gather_copy(j, 0).start()

        twin_copy(j, tp).start()

    def forward(k):
        j = nth(k)
        paired = k <= 2 * both

        @pl.when((k > 0) & jnp.logical_not(paired & (k % 2 == 0)))
        def _():
            arrive(j)

        @pl.when((k % 2 == 1) & (k + 1 <= 2 * both))
        def _():
            arrive(nth(k + 1))

        twin_copy(j, sib).wait_recv()
        xdy_store(j).start()
        rows = pair(j)
        for i, (weight, first) in enumerate(((wg, 0), (wu, 0), (wd, width))):
            @pl.when(k == 0)
            def _():
                loads[2 + i].wait()

            block = xdy[rows, first:first + width]
            for at in range(0, ff, ff_tile):
                out = dot(block, weight[at:at + ff_tile, :], (1, 1))
                part[i, rows, at:at + ff_tile] = out
                psend[i, rows, at:at + ff_tile] = out.astype(BF16)
            for step in range(1, n_exp):
                partial_copy(j, i, step).start()

    def backward(k):
        j = nth(k)
        rows = pair(j)
        slot = k % 2
        for i in range(3):
            for step in range(1, n_exp):
                partial_copy(j, i, step).wait_recv()
        share = xdy[rows, 2 * width:2 * width + 1].astype(F32)
        score = jnp.zeros((PAIR, 1), F32)
        for at in range(0, ff, ff_tile):
            sums = []
            for i in range(3):
                total = part[i, rows, at:at + ff_tile]
                for step in range(1, n_exp):
                    total = total + precv[step - 1, i, rows, at:at + ff_tile].astype(F32)
                sums.append(total)
            gate_pre, up_pre, back = sums
            sig = jax.nn.sigmoid(gate_pre)
            activated = gate_pre * sig
            hidden = (activated * up_pre).astype(BF16).astype(F32)
            score = score + jnp.sum(hidden * back, axis=1, keepdims=True)
            shared = share * back
            act[rows, at:at + ff_tile] = (
                shared * up_pre * sig * (1.0 + gate_pre * (1.0 - sig))
            ).astype(BF16)
            act[rows, ff + at:ff + at + ff_tile] = (shared * activated).astype(BF16)
            act[rows, 2 * ff + at:2 * ff + at + ff_tile] = (share * hidden).astype(BF16)
        act_store(j).start()
        gate_back, up_back = act[rows, 0:ff], act[rows, ff:2 * ff]
        for at in range(0, width, col_tile):
            grad[slot, :, at:at + col_tile] = dot(gate_back, wg[:, at:at + col_tile], (1, 0)) + dot(
                up_back, wu[:, at:at + col_tile], (1, 0)
            )
        grad[slot, :, width:] = jnp.broadcast_to(score, (PAIR, LANES))

        theirs = block_half(sib)
        sib_out[j, :, 0:width] = grad[slot, theirs, 0:width].astype(BF16)
        high, low = split_score(grad[slot, theirs, width:])
        sib_out[j, :, width:width + LANES] = high
        sib_out[j, :, width + LANES:] = low
        pair_sum_copy(j).start()

    def finish(k):
        j = nth(k)
        slot, ours = k % 2, block_half(tp)
        pair_sum_copy(j).wait_recv()
        main = grad[slot, ours, 0:width] + sib_in[j, :, 0:width].astype(F32)
        total = (
            grad[slot, ours, width:]
            + sib_in[j, :, width:width + LANES].astype(F32)
            + sib_in[j, :, width + LANES:].astype(F32)
        )

        @pl.when(j == c)
        def _():
            acc[:, 0:width] = main
            acc[:, width:] = total

        @pl.when(j != c)
        def _():
            rs_out[j, :, 0:width] = main.astype(BF16)
            high, low = split_score(total)
            rs_out[j, :, width:width + LANES] = high
            rs_out[j, :, width + LANES:] = low
            home_copy(j, c).start()

    @pl.loop(0, n)
    def _(k):
        forward(k)

    @pl.loop(0, n + 1)
    def _(k):
        @pl.when(k >= 1)
        def _():
            finish(k - 1)

        @pl.when(k < n)
        def _():
            backward(k)

    @pl.loop(0, n)
    def _(j):
        @pl.when(j != c)
        def _():
            home_copy(j, j).wait_recv()
            acc[:, 0:width] += rs_in[j, :, 0:width].astype(F32)
            acc[:, width:] += rs_in[j, :, width:width + LANES].astype(F32) + rs_in[
                j, :, width + LANES:
            ].astype(F32)

    sg_ref[...] = acc[:, 0:width].astype(BF16)
    score_ref[...] = acc[:, width:]

    @pl.loop(0, n)
    def _(j):
        @pl.when((j <= c) & (c + 1 < n))
        def _():
            gather_copy(j, 1).wait_send()

        @pl.when((j >= c) & (c > 0))
        def _():
            gather_copy(j, 0).wait_send()

        twin_copy(j, tp).wait_send()
        for i in range(3):
            for step in range(1, n_exp):
                partial_copy(j, i, step).wait_send()
        pair_sum_copy(j).wait_send()

        @pl.when(j != c)
        def _():
            home_copy(j, c).wait_send()

        xdy_store(j).wait()
        act_store(j).wait()


def exchange(n, n_exp, ids, logits, tokens, cotangent, w_gate, w_up, w_down):
    rows, width = tokens.shape
    ff = w_gate.shape[0]
    slots = n * PAIR
    wide = 2 * width + LANES
    home = width + 2 * LANES
    vmem = pl.BlockSpec(memory_space=pltpu.VMEM)
    hbm = pl.BlockSpec(memory_space=pl.ANY)
    dma = pltpu.SemaphoreType.DMA
    return pl.pallas_call(
        functools.partial(exchange_kernel, n, n_exp),
        out_shape=(
            jax.ShapeDtypeStruct((slots, wide), BF16),
            jax.ShapeDtypeStruct((slots, 3 * ff), BF16),
            jax.ShapeDtypeStruct((CAP, width), BF16),
            jax.ShapeDtypeStruct((CAP, LANES), F32),
        ),
        in_specs=[vmem, vmem] + [hbm] * 5,
        out_specs=(hbm, hbm, vmem, vmem),
        scratch_shapes=[
            pltpu.VMEM((rows, width), BF16),
            pltpu.VMEM((rows, width), BF16),
            pltpu.VMEM((ff, width), BF16),
            pltpu.VMEM((ff, width), BF16),
            pltpu.VMEM((ff, width), BF16),
            pltpu.VMEM((slots, wide), BF16),
            pltpu.VMEM((3, slots, ff), F32),
            pltpu.VMEM((3, slots, ff), BF16),
            pltpu.VMEM((n_exp - 1, 3, slots, ff), BF16),
            pltpu.VMEM((slots, 3 * ff), BF16),
            pltpu.VMEM((2, PAIR, width + LANES), F32),
            pltpu.VMEM((n, CAP, home), BF16),
            pltpu.VMEM((n, CAP, home), BF16),
            pltpu.VMEM((n, CAP, home), BF16),
            pltpu.VMEM((n, CAP, home), BF16),
            pltpu.VMEM((CAP, width + LANES), F32),
            dma((5,)),
            dma((n, 2)),
            dma((n,)),
            dma((n,)),
            dma((n,)),
            dma((n_exp - 1, 3, n)),
            dma((n_exp - 1, 3, n)),
            dma((n,)),
            dma((n,)),
            dma((n,)),
            dma((n,)),
            dma((n,)),
            dma((n,)),
        ],
        compiler_params=pltpu.CompilerParams(
            collective_id=0, has_side_effects=True, vmem_limit_bytes=56 * 1024 * 1024
        ),
    )(ids, logits, tokens, cotangent, w_gate, w_up, w_down)


def grads_kernel(
    ids_ref, logits_ref, score_ref, sg_ref, act_ref, x_ref, dy_ref,
    token_grad, logit_grad, gate_grad, up_grad, down_grad, turned, pick_ref,
):
    ff = gate_grad.shape[0]

    @pl.when(pl.program_id(0) == 0)
    def _():
        pick, hits, shares = routing(ids_ref, logits_ref)
        pick_ref[...] = pick.astype(BF16)
        token_score = jnp.sum(pick * score_ref[:, 0:1], axis=0, keepdims=True)
        terms = [jnp.where(hit, token_score, 0.0) for hit in hits]
        mean = shares[0] * terms[0] + shares[1] * terms[1]
        logit_grad[0:1, :] = shares[0] * (terms[0] - mean)
        logit_grad[1:2, :] = shares[1] * (terms[1] - mean)
        for at in range(0, 3 * ff, 256):
            turned[at:at + 256, :] = act_ref[:, at:at + 256].T

    x, dy = x_ref[...], dy_ref[...]
    gate_grad[...] = dot(turned[0:ff, :], x, (1, 0)).astype(BF16)
    up_grad[...] = dot(turned[ff:2 * ff, :], x, (1, 0)).astype(BF16)
    down_grad[...] = dot(turned[2 * ff:, :], dy, (1, 0)).astype(BF16)
    token_grad[...] = dot(pick_ref[...], sg_ref[...], (0, 0)).astype(BF16)


def grads(ids, logits, score, slot_grad, act, xdy, width):
    slots = act.shape[0]
    ff = act.shape[1] // 3
    rows = ids.shape[1]
    tile = 512 if width % 512 == 0 else 256
    tiles = width // tile

    def whole(shape):
        return pl.BlockSpec(shape, lambda i: (0, 0))

    def column(height, shift=0):
        return pl.BlockSpec((height, tile), lambda i: (0, i + shift))

    return pl.pallas_call(
        grads_kernel,
        grid=(tiles,),
        out_shape=(
            jax.ShapeDtypeStruct((rows, width), BF16),
            jax.ShapeDtypeStruct((2, rows), F32),
            jax.ShapeDtypeStruct((ff, width), BF16),
            jax.ShapeDtypeStruct((ff, width), BF16),
            jax.ShapeDtypeStruct((ff, width), BF16),
        ),
        in_specs=[
            whole((2, rows)),
            whole((2, rows)),
            whole((CAP, LANES)),
            column(CAP),
            whole((slots, 3 * ff)),
            column(slots),
            column(slots, tiles),
        ],
        out_specs=(column(rows), whole((2, rows)), column(ff), column(ff), column(ff)),
        scratch_shapes=[pltpu.VMEM((3 * ff, slots), BF16), pltpu.VMEM((CAP, rows), BF16)],
        compiler_params=pltpu.CompilerParams(vmem_limit_bytes=60 * 1024 * 1024),
    )(ids, logits, score, slot_grad, act, xdy, xdy)


def solution(mesh):
    n, n_exp = mesh.shape["ctx"], mesh.shape["exp"]

    def shards(tokens, cotangent, route_logits, expert_ids, w_gate, w_up, w_down):
        ids, logits = expert_ids.T, route_logits.T
        xdy, act, slot_grad, score = exchange(
            n, n_exp, ids, logits, tokens, cotangent, w_gate, w_up, w_down
        )
        token_grad, logit_grad, gate_grad, up_grad, down_grad = grads(
            ids, logits, score, slot_grad, act, xdy, tokens.shape[1]
        )
        return token_grad, logit_grad.T, gate_grad, up_grad, down_grad

    features = P(("groups", "ctx", "tp"), "exp")
    routes = P(("groups", "ctx", "tp"), None)
    weights = P(("ctx", "tp"), "exp")
    return jax.shard_map(
        shards,
        mesh=mesh,
        in_specs=(features, features, routes, routes, weights, weights, weights),
        out_specs=(features, routes, features, features, features),
        check_vma=False,
    )
```

```python
import functools

import jax
import jax.numpy as jnp
from jax import lax
from jax.experimental import pallas as pl
from jax.experimental.pallas import tpu as pltpu
from jax.sharding import PartitionSpec as P

CAP = 32
PAIR = 2 * CAP
LANES = 128
MESH = pl.DeviceIdType.MESH
F32 = jnp.float32
BF16 = jnp.bfloat16


def dot(left, right, contract):
    return lax.dot_general(
        left, right, ((contract[:1], contract[1:]), ((), ())), preferred_element_type=F32
    )


def routing(ids_ref, logits_ref):
    tokens = ids_ref.shape[1]
    hit_0, hit_1 = ids_ref[0:1, :] == 0, ids_ref[1:2, :] == 0
    chosen = jnp.where(hit_0 | hit_1, 1.0, 0.0)
    earlier = lax.broadcasted_iota(jnp.int32, (tokens, tokens), 0) < lax.broadcasted_iota(
        jnp.int32, (tokens, tokens), 1
    )
    position = dot(
        jnp.broadcast_to(chosen, (16, tokens)).astype(BF16),
        jnp.where(earlier, 1.0, 0.0).astype(BF16),
        (1, 0),
    )[0:1, :]
    slot = lax.broadcasted_iota(jnp.int32, (CAP, tokens), 0).astype(F32)
    pick = jnp.where(slot == position, 1.0, 0.0) * chosen
    gap = logits_ref[0:1, :] - logits_ref[1:2, :]
    return pick, (hit_0, hit_1), (jax.nn.sigmoid(gap), jax.nn.sigmoid(-gap))


def split_score(score):
    high = score.astype(BF16)
    return high, (score - high.astype(F32)).astype(BF16)


def exchange_kernel(
    n, n_exp,
    ids_ref, logits_ref, tok_hbm, cot_hbm, wg_hbm, wu_hbm, wd_hbm,
    xdy_out, act_out, sg_ref, score_ref,
    tok, cot, wg, wu, wd, xdy, psend, precv, act, grad, sib_out, sib_in, rs_out, rs_in, acc,
    load_sem, ag_send, ag_recv, sib_send, sib_recv, x_send, x_recv,
    gs_send, gs_recv, rs_send, rs_recv, xo_sem, ao_sem,
):
    c, e, tp = lax.axis_index("ctx"), lax.axis_index("exp"), lax.axis_index("tp")
    sib = 1 - tp
    width = wg.shape[1]
    ff = wg.shape[0]
    ff_tile = min(ff, 256)
    col_tile = 512 if width % 512 == 0 else 256

    loads = [
        pltpu.make_async_copy(src, dst, load_sem.at[i])
        for i, (src, dst) in enumerate(
            ((tok_hbm, tok), (cot_hbm, cot), (wg_hbm, wg), (wu_hbm, wu), (wd_hbm, wd))
        )
    ]
    for load in loads[:2]:
        load.start()

    barrier = pltpu.get_barrier_semaphore()
    for step in range(1, n):
        pl.semaphore_signal(
            barrier, inc=1, device_id={"ctx": lax.rem(c + step, n)}, device_id_type=MESH
        )
    for step in range(1, n_exp):
        pl.semaphore_signal(
            barrier, inc=1, device_id={"exp": lax.rem(e + step, n_exp)}, device_id_type=MESH
        )
    pl.semaphore_signal(barrier, inc=1, device_id={"tp": sib}, device_id_type=MESH)

    def half(j, which):
        return pl.ds(pl.multiple_of(j * PAIR + which * CAP, CAP), CAP)

    def pair(j):
        return pl.ds(pl.multiple_of(j * PAIR, PAIR), PAIR)

    def block_half(which):
        return pl.ds(pl.multiple_of(which * CAP, CAP), CAP)

    def gather_copy(j, side):
        to = jnp.where(c + 1 < n, c + 1, 0) if side == 1 else jnp.where(c > 0, c - 1, n - 1)
        return pltpu.make_async_remote_copy(
            src_ref=xdy.at[half(j, tp)], dst_ref=xdy.at[half(j, tp)],
            send_sem=ag_send.at[j, side], recv_sem=ag_recv.at[j],
            device_id={"ctx": to}, device_id_type=MESH,
        )

    def twin_copy(j, which):
        return pltpu.make_async_remote_copy(
            src_ref=xdy.at[half(j, which)], dst_ref=xdy.at[half(j, which)],
            send_sem=sib_send.at[j], recv_sem=sib_recv.at[j],
            device_id={"tp": sib}, device_id_type=MESH,
        )

    def partial_copy(j, i, step):
        return pltpu.make_async_remote_copy(
            src_ref=psend.at[i, pair(j)], dst_ref=precv.at[step - 1, i, pair(j)],
            send_sem=x_send.at[step - 1, i, j], recv_sem=x_recv.at[step - 1, i, j],
            device_id={"exp": lax.rem(e + step, n_exp)}, device_id_type=MESH,
        )

    def pair_sum_copy(j):
        return pltpu.make_async_remote_copy(
            src_ref=sib_out.at[j], dst_ref=sib_in.at[j],
            send_sem=gs_send.at[j], recv_sem=gs_recv.at[j],
            device_id={"tp": sib}, device_id_type=MESH,
        )

    def home_copy(j, source):
        return pltpu.make_async_remote_copy(
            src_ref=rs_out.at[j], dst_ref=rs_in.at[source],
            send_sem=rs_send.at[j], recv_sem=rs_recv.at[source],
            device_id={"ctx": j}, device_id_type=MESH,
        )

    def xdy_store(j):
        return pltpu.make_async_copy(xdy.at[pair(j)], xdy_out.at[pair(j)], xo_sem.at[j])

    def act_store(j):
        return pltpu.make_async_copy(act.at[pair(j)], act_out.at[pair(j)], ao_sem.at[j])

    pick, hits, shares = routing(ids_ref, logits_ref)
    token_share = jnp.where(hits[0], shares[0], 0.0) + jnp.where(hits[1], shares[1], 0.0)
    token_share = token_share.astype(BF16).astype(F32)
    share = jnp.sum(pick * token_share, axis=1, keepdims=True)
    mine = half(c, tp)
    xdy[mine, 2 * width:] = jnp.broadcast_to(share, (CAP, LANES)).astype(BF16)
    pick = pick.astype(BF16)
    for which, ref in enumerate((tok, cot)):
        loads[which].wait()
        for at in range(0, width, col_tile):
            xdy[mine, which * width + at:which * width + at + col_tile] = dot(
                pick, ref[:, at:at + col_tile], (1, 0)
            ).astype(BF16)

    for load in loads[2:]:
        load.start()
    pl.semaphore_wait(barrier, n + n_exp - 1)

    @pl.when(c + 1 < n)
    def _():
        gather_copy(c, 1).start()

    @pl.when(c > 0)
    def _():
        gather_copy(c, 0).start()

    twin_copy(c, tp).start()

    both = jnp.where(2 * c <= n - 1, c, n - 1 - c)

    def nth(k):
        near = c + jnp.where(k % 2 == 0, 1, -1) * ((k + 1) // 2)
        far = jnp.where(2 * c <= n - 1, k, n - 1 - k)
        return jnp.where(k <= 2 * both, near, far)

    def arrive(j):
        gather_copy(j, 1).wait_recv()

        @pl.when((j < c) & (c + 1 < n))
        def _():
            gather_copy(j, 1).start()

        @pl.when((j > c) & (c > 0))
        def _():
            gather_copy(j, 0).start()

        twin_copy(j, tp).start()

    def forward(k):
        j = nth(k)
        second = (k >= 2) & (k % 2 == 0) & (k <= 2 * both)

        @pl.when((k == 1) | ((k > 2 * both) & (k >= 2) & (k != 2 * both + 1)))
        def _():
            arrive(j)

        @pl.when((k == 1) & (2 <= 2 * both))
        def _():
            arrive(nth(k + 1))

        @pl.when(second & (k + 1 < n))
        def _():
            arrive(nth(k + 1))

        @pl.when(second & (k + 2 <= 2 * both))
        def _():
            arrive(nth(k + 2))

        twin_copy(j, sib).wait_recv()
        xdy_store(j).start()
        rows = pair(j)
        for i, (weight, first) in enumerate(((wg, 0), (wu, 0), (wd, width))):
            @pl.when(k == 0)
            def _():
                loads[2 + i].wait()

            block = xdy[rows, first:first + width]
            for at in range(0, ff, ff_tile):
                out = dot(block, weight[at:at + ff_tile, :], (1, 1))
                psend[i, rows, at:at + ff_tile] = out.astype(BF16)
            for step in range(1, n_exp):
                partial_copy(j, i, step).start()

    def backward(k):
        j = nth(k)
        rows = pair(j)
        slot = k % 2
        for i in range(3):
            for step in range(1, n_exp):
                partial_copy(j, i, step).wait_recv()
        share = xdy[rows, 2 * width:2 * width + 1].astype(F32)
        score = jnp.zeros((PAIR, 1), F32)
        for at in range(0, ff, ff_tile):
            sums = []
            for i in range(3):
                total = psend[i, rows, at:at + ff_tile].astype(F32)
                for step in range(1, n_exp):
                    total = total + precv[step - 1, i, rows, at:at + ff_tile].astype(F32)
                sums.append(total)
            gate_pre, up_pre, back = sums
            sig = jax.nn.sigmoid(gate_pre)
            activated = gate_pre * sig
            hidden = (activated * up_pre).astype(BF16).astype(F32)
            score = score + jnp.sum(hidden * back, axis=1, keepdims=True)
            shared = share * back
            act[rows, at:at + ff_tile] = (
                shared * up_pre * sig * (1.0 + gate_pre * (1.0 - sig))
            ).astype(BF16)
            act[rows, ff + at:ff + at + ff_tile] = (shared * activated).astype(BF16)
            act[rows, 2 * ff + at:2 * ff + at + ff_tile] = (share * hidden).astype(BF16)
        act_store(j).start()
        gate_back, up_back = act[rows, 0:ff], act[rows, ff:2 * ff]
        for at in range(0, width, col_tile):
            grad[slot, :, at:at + col_tile] = dot(gate_back, wg[:, at:at + col_tile], (1, 0)) + dot(
                up_back, wu[:, at:at + col_tile], (1, 0)
            )
        grad[slot, :, width:] = jnp.broadcast_to(score, (PAIR, LANES))

        theirs = block_half(sib)
        sib_out[j, :, 0:width] = grad[slot, theirs, 0:width].astype(BF16)
        high, low = split_score(grad[slot, theirs, width:])
        sib_out[j, :, width:width + LANES] = high
        sib_out[j, :, width + LANES:] = low
        pair_sum_copy(j).start()

    def finish(k):
        j = nth(k)
        slot, ours = k % 2, block_half(tp)
        pair_sum_copy(j).wait_recv()
        main = grad[slot, ours, 0:width] + sib_in[j, :, 0:width].astype(F32)
        total = (
            grad[slot, ours, width:]
            + sib_in[j, :, width:width + LANES].astype(F32)
            + sib_in[j, :, width + LANES:].astype(F32)
        )

        @pl.when(j == c)
        def _():
            acc[:, 0:width] = main
            acc[:, width:] = total

        @pl.when(j != c)
        def _():
            rs_out[j, :, 0:width] = main.astype(BF16)
            high, low = split_score(total)
            rs_out[j, :, width:width + LANES] = high
            rs_out[j, :, width + LANES:] = low
            home_copy(j, c).start()

    @pl.loop(0, n + 2)
    def _(k):
        @pl.when(k < n)
        def _():
            forward(k)

        @pl.when(k >= 2)
        def _():
            finish(k - 2)

        @pl.when((k >= 1) & (k <= n))
        def _():
            backward(k - 1)

    @pl.loop(0, n)
    def _(j):
        @pl.when(j != c)
        def _():
            home_copy(j, j).wait_recv()
            acc[:, 0:width] += rs_in[j, :, 0:width].astype(F32)
            acc[:, width:] += rs_in[j, :, width:width + LANES].astype(F32) + rs_in[
                j, :, width + LANES:
            ].astype(F32)

    sg_ref[...] = acc[:, 0:width].astype(BF16)
    score_ref[...] = acc[:, width:]

    @pl.loop(0, n)
    def _(j):
        @pl.when((j <= c) & (c + 1 < n))
        def _():
            gather_copy(j, 1).wait_send()

        @pl.when((j >= c) & (c > 0))
        def _():
            gather_copy(j, 0).wait_send()

        twin_copy(j, tp).wait_send()
        for i in range(3):
            for step in range(1, n_exp):
                partial_copy(j, i, step).wait_send()
        pair_sum_copy(j).wait_send()

        @pl.when(j != c)
        def _():
            home_copy(j, c).wait_send()

        xdy_store(j).wait()
        act_store(j).wait()


def exchange(n, n_exp, ids, logits, tokens, cotangent, w_gate, w_up, w_down):
    rows, width = tokens.shape
    ff = w_gate.shape[0]
    slots = n * PAIR
    wide = 2 * width + LANES
    home = width + 2 * LANES
    vmem = pl.BlockSpec(memory_space=pltpu.VMEM)
    hbm = pl.BlockSpec(memory_space=pl.ANY)
    dma = pltpu.SemaphoreType.DMA
    return pl.pallas_call(
        functools.partial(exchange_kernel, n, n_exp),
        out_shape=(
            jax.ShapeDtypeStruct((slots, wide), BF16),
            jax.ShapeDtypeStruct((slots, 3 * ff), BF16),
            jax.ShapeDtypeStruct((CAP, width), BF16),
            jax.ShapeDtypeStruct((CAP, LANES), F32),
        ),
        in_specs=[vmem, vmem] + [hbm] * 5,
        out_specs=(hbm, hbm, vmem, vmem),
        scratch_shapes=[
            pltpu.VMEM((rows, width), BF16),
            pltpu.VMEM((rows, width), BF16),
            pltpu.VMEM((ff, width), BF16),
            pltpu.VMEM((ff, width), BF16),
            pltpu.VMEM((ff, width), BF16),
            pltpu.VMEM((slots, wide), BF16),
            pltpu.VMEM((3, slots, ff), BF16),
            pltpu.VMEM((n_exp - 1, 3, slots, ff), BF16),
            pltpu.VMEM((slots, 3 * ff), BF16),
            pltpu.VMEM((2, PAIR, width + LANES), F32),
            pltpu.VMEM((n, CAP, home), BF16),
            pltpu.VMEM((n, CAP, home), BF16),
            pltpu.VMEM((n, CAP, home), BF16),
            pltpu.VMEM((n, CAP, home), BF16),
            pltpu.VMEM((CAP, width + LANES), F32),
            dma((5,)),
            dma((n, 2)),
            dma((n,)),
            dma((n,)),
            dma((n,)),
            dma((n_exp - 1, 3, n)),
            dma((n_exp - 1, 3, n)),
            dma((n,)),
            dma((n,)),
            dma((n,)),
            dma((n,)),
            dma((n,)),
            dma((n,)),
        ],
        compiler_params=pltpu.CompilerParams(
            collective_id=0, has_side_effects=True, vmem_limit_bytes=56 * 1024 * 1024
        ),
    )(ids, logits, tokens, cotangent, w_gate, w_up, w_down)


def grads_kernel(
    ids_ref, logits_ref, score_ref, sg_ref, act_ref, x_ref, dy_ref,
    token_grad, logit_grad, gate_grad, up_grad, down_grad, turned, pick_ref,
):
    ff = gate_grad.shape[0]

    @pl.when(pl.program_id(0) == 0)
    def _():
        pick, hits, shares = routing(ids_ref, logits_ref)
        pick_ref[...] = pick.astype(BF16)
        token_score = jnp.sum(pick * score_ref[:, 0:1], axis=0, keepdims=True)
        terms = [jnp.where(hit, token_score, 0.0) for hit in hits]
        mean = shares[0] * terms[0] + shares[1] * terms[1]
        logit_grad[0:1, :] = shares[0] * (terms[0] - mean)
        logit_grad[1:2, :] = shares[1] * (terms[1] - mean)
        for at in range(0, 3 * ff, 256):
            turned[at:at + 256, :] = act_ref[:, at:at + 256].T

    x, dy = x_ref[...], dy_ref[...]
    gate_grad[...] = dot(turned[0:ff, :], x, (1, 0)).astype(BF16)
    up_grad[...] = dot(turned[ff:2 * ff, :], x, (1, 0)).astype(BF16)
    down_grad[...] = dot(turned[2 * ff:, :], dy, (1, 0)).astype(BF16)
    token_grad[...] = dot(pick_ref[...], sg_ref[...], (0, 0)).astype(BF16)


def grads(ids, logits, score, slot_grad, act, xdy, width):
    slots = act.shape[0]
    ff = act.shape[1] // 3
    rows = ids.shape[1]
    tile = 256
    tiles = width // tile

    def whole(shape):
        return pl.BlockSpec(shape, lambda i: (0, 0))

    def column(height, shift=0):
        return pl.BlockSpec((height, tile), lambda i: (0, i + shift))

    return pl.pallas_call(
        grads_kernel,
        grid=(tiles,),
        out_shape=(
            jax.ShapeDtypeStruct((rows, width), BF16),
            jax.ShapeDtypeStruct((2, rows), F32),
            jax.ShapeDtypeStruct((ff, width), BF16),
            jax.ShapeDtypeStruct((ff, width), BF16),
            jax.ShapeDtypeStruct((ff, width), BF16),
        ),
        in_specs=[
            whole((2, rows)),
            whole((2, rows)),
            whole((CAP, LANES)),
            column(CAP),
            whole((slots, 3 * ff)),
            column(slots),
            column(slots, tiles),
        ],
        out_specs=(column(rows), whole((2, rows)), column(ff), column(ff), column(ff)),
        scratch_shapes=[pltpu.VMEM((3 * ff, slots), BF16), pltpu.VMEM((CAP, rows), BF16)],
        compiler_params=pltpu.CompilerParams(vmem_limit_bytes=60 * 1024 * 1024),
    )(ids, logits, score, slot_grad, act, xdy, xdy)


def solution(mesh):
    n, n_exp = mesh.shape["ctx"], mesh.shape["exp"]

    def shards(tokens, cotangent, route_logits, expert_ids, w_gate, w_up, w_down):
        ids, logits = expert_ids.T, route_logits.T
        xdy, act, slot_grad, score = exchange(
            n, n_exp, ids, logits, tokens, cotangent, w_gate, w_up, w_down
        )
        token_grad, logit_grad, gate_grad, up_grad, down_grad = grads(
            ids, logits, score, slot_grad, act, xdy, tokens.shape[1]
        )
        return token_grad, logit_grad.T, gate_grad, up_grad, down_grad

    features = P(("groups", "ctx", "tp"), "exp")
    routes = P(("groups", "ctx", "tp"), None)
    weights = P(("ctx", "tp"), "exp")
    return jax.shard_map(
        shards,
        mesh=mesh,
        in_specs=(features, features, routes, routes, weights, weights, weights),
        out_specs=(features, routes, features, features, features),
        check_vma=False,
    )
```
